32 devices in a mesh: blk: 16 (over z, y, core), copy: 2 (over x).
Axes of the slice: x: 2, y: 2, z: 4, core: 2. Of those that a mesh axis runs over, the one named last changes fastest.
Arguments:
- features: float32 [4096, 512], P(('blk', 'copy')), may hold values from -16 to 16
- attend_source: float32 [8, 64], replicated, may hold values from -1 to 1
- attend_target: float32 [8, 64], replicated, may hold values from -1 to 1
- key_blocks: int32 [32, 6], P(('blk', 'copy')), may hold values from 0 to 31, as said below
- live_slots: int32 [32], P(('blk', 'copy')), may hold values from 3 to 6, as said below
- edge_bits: int32 [32, 6, 16, 128], P(('blk', 'copy')), may hold values from 0 to 255
- cotangent: float32 [4096, 512], P(('blk', 'copy')), may hold values from -6 to 6
Outputs:
- layer_out: float32 [4096, 512], P(('blk', 'copy'))
- feature_grad: float32 [4096, 512], P(('blk', 'copy'))
- source_grad: float32 [8, 64], replicated
- target_grad: float32 [8, 64], replicated
The draws below stay inside these ranges and needn't reach their ends.
Inputs may be any that keep to these rules, and one draw needn't show every extreme that they name: `key_blocks`: slot 0 of query block q holds q itself. The other slots hold distinct blocks, each in the panel of q (the 2 blocks b with b // 2 equal to q // 2) or in one of the two panels beside it, panel numbers taken modulo 32 // 2; slot 1 lies in the panel before and slot 2 in the panel after. `live_slots`: some query block uses all 6 slots.
All inputs are finite; a program needn't handle non-finite values.
Results may differ from the reference program's by a relative error of at most 0.0003.
Values sent between devices are 32-bit elements; how exact they have to be, the bound alone decides.
A program may use at most 64 MiB of HBM per device.

```python
import jax
import jax.numpy as jnp
from jax import lax

H = 8
C = 64
D = 512
BLOCK = 128
NNZ = 6
PANEL_BLOCKS = 2
QBLOCKS = 32
NODES = 4096


def head_spread(key, low, high):
    level = jax.random.uniform(key, (H, 1), jnp.float32)
    return low * jnp.exp(level * jnp.log(high / low))


def target_vector(key):
    sub_key = jax.random.fold_in(key, 101)
    spread = head_spread(jax.random.fold_in(key, 102), 0.4, 2.5)
    return jnp.clip(jax.random.normal(sub_key, (H, C), jnp.float32) * 0.125 * spread, -1.0, 1.0)


def draw_attend_target(key, part):
    return target_vector(key)


def draw_attend_source(key, part):
    sub_key = jax.random.fold_in(key, 103)
    spread = head_spread(jax.random.fold_in(key, 104), 0.4, 2.5)
    base = jax.random.normal(sub_key, (H, C), jnp.float32)
    return jnp.clip(base * 0.125 * spread, -1.0, 1.0)


def draw_features(key, part):
    base_key = jax.random.fold_in(key, 201)
    row_key = jax.random.fold_in(key, 202)
    row_scale = 0.4 * jnp.exp(jax.random.uniform(row_key, (NODES, 1), jnp.float32) * jnp.log(10.0))
    base = jax.random.normal(base_key, (NODES, H * C), jnp.float32) * row_scale
    return jnp.clip(base, -16.0, 16.0)


def draw_key_blocks(key, part):
    order_key = jax.random.fold_in(key, 301)
    left_key = jax.random.fold_in(key, 302)
    right_key = jax.random.fold_in(key, 303)
    panel_count = QBLOCKS // PANEL_BLOCKS
    block_index = jnp.arange(QBLOCKS, dtype=jnp.int32)
    panel_index = block_index // PANEL_BLOCKS
    inner_index = block_index % PANEL_BLOCKS
    cand_count = 3 * PANEL_BLOCKS - 1
    cand_index = jnp.arange(cand_count, dtype=jnp.int32)[None, :]
    ranking = jax.random.randint(order_key, (QBLOCKS, cand_count), 0, 1048576) * cand_count + cand_index
    left_pick = jax.random.randint(left_key, (QBLOCKS, 1), 0, PANEL_BLOCKS)
    right_pick = jax.random.randint(right_key, (QBLOCKS, 1), 0, PANEL_BLOCKS) + 2 * PANEL_BLOCKS - 1
    ranking = jnp.where(cand_index == left_pick, -2, ranking)
    ranking = jnp.where(cand_index == right_pick, -1, ranking)
    chosen = jnp.argsort(ranking, axis=1, stable=True)[:, :NNZ - 1].astype(jnp.int32)
    before = jnp.mod(panel_index - 1, panel_count)[:, None] * PANEL_BLOCKS + chosen
    within_index = chosen - PANEL_BLOCKS
    within = panel_index[:, None] * PANEL_BLOCKS + within_index + (within_index >= inner_index[:, None]).astype(jnp.int32)
    after = jnp.mod(panel_index + 1, panel_count)[:, None] * PANEL_BLOCKS + chosen - (2 * PANEL_BLOCKS - 1)
    mapped = jnp.where(chosen < PANEL_BLOCKS, before, jnp.where(chosen < 2 * PANEL_BLOCKS - 1, within, after))
    return jnp.concatenate([block_index[:, None], mapped], axis=1).astype(jnp.int32)


def draw_live_slots(key, part):
    spread = max(NNZ - 3, 1)
    first_draw = jax.random.randint(jax.random.fold_in(key, 401), (QBLOCKS,), 0, NNZ - 2)
    second_draw = jax.random.randint(jax.random.fold_in(key, 402), (QBLOCKS,), 0, NNZ - 2)
    live_count = 3 + first_draw * second_draw // spread
    full_block = jax.random.randint(jax.random.fold_in(key, 403), (), 0, QBLOCKS)
    return jnp.where(jnp.arange(QBLOCKS) == full_block, NNZ, live_count).astype(jnp.int32)


def plant(entries, stream_key, low, largest):
    spot = [jax.random.randint(jax.random.fold_in(stream_key, axis), (), 0, length) for axis, length in enumerate(entries.shape)]
    longest = entries.shape.index(max(entries.shape))
    beside = spot[:longest] + [(spot[longest] + 1) % entries.shape[longest]] + spot[longest + 1:]
    return entries.at[tuple(spot)].set(low).at[tuple(beside)].set(largest)


def shard_levels(own_key, extent, pieces, least, largest):
    loudness, own = 1.0, jax.random.fold_in(own_key, 6)
    for position, shards_of in pieces:
        heights = jnp.exp(jax.random.uniform(jax.random.fold_in(own, position), (shards_of,), jnp.float32, least / len(pieces), largest / len(pieces)))
        loudness = loudness * jnp.repeat(heights, extent[position] // shards_of).reshape([-1 if axis == position else 1 for axis in range(len(extent))])
    return loudness


def gaussian(key, extent, scale, bound, shards=(), kind=jnp.bfloat16):
    result = jax.random.normal(key, extent, jnp.float32) * scale
    if len(shards) > 0:
        result = shard_levels(key, extent, shards, -0.22, 0.18) * result
    return jnp.clip(result, min=-bound, max=bound).astype(kind)


def setup_inputs(seed: int = 0) -> dict:
    keys = jax.random.split(jax.random.key(seed), 8)
    features = draw_features(jax.random.fold_in(keys[7], 71), 0)
    attend_source = draw_attend_source(jax.random.fold_in(keys[7], 71), 0)
    attend_target = draw_attend_target(jax.random.fold_in(keys[7], 71), 0)
    key_blocks = draw_key_blocks(jax.random.fold_in(keys[7], 71), 0)
    live_slots = draw_live_slots(jax.random.fold_in(keys[7], 71), 0)
    edge_bits = plant(jax.random.randint(keys[5], (QBLOCKS, NNZ, BLOCK // 8, BLOCK), 0, 256), jax.random.fold_in(keys[5], 1), 0, 255).astype(jnp.int32)
    cotangent = gaussian(keys[6], (NODES, D), 1.0, 6.0, ((0, 32),), jnp.float32)
    return dict(features=features, attend_source=attend_source, attend_target=attend_target, key_blocks=key_blocks, live_slots=live_slots, edge_bits=edge_bits, cotangent=cotangent)


precise = lax.Precision.HIGHEST


def add_rows(panel, piece, row_start):
    current = lax.dynamic_slice_in_dim(panel, row_start, piece.shape[0], 0)
    return lax.dynamic_update_slice_in_dim(panel, current + piece, row_start, 0)


def reference(features, attend_source, attend_target, key_blocks, live_slots, edge_bits, cotangent):
    head_count, head_width = attend_source.shape
    node_count, model_width = features.shape
    block_count, slot_count = key_blocks.shape
    block_rows = node_count // block_count
    bit_shift = jnp.arange(8, dtype=jnp.int32)
    diagonal = jnp.arange(block_rows)[:, None] == jnp.arange(block_rows)[None, :]
    slot_range = jnp.arange(slot_count, dtype=jnp.int32)

    def per_block(loop_state, block_index):
        feature_grad, source_att, target_att = loop_state
        row_start = (block_index * block_rows).astype(jnp.int32)
        query_rows = lax.dynamic_slice_in_dim(features, row_start, block_rows, 0)
        query_values = query_rows.reshape(block_rows, head_count, head_width)
        block_ids = lax.dynamic_index_in_dim(key_blocks, block_index, 0, keepdims=False)
        live_count = lax.dynamic_index_in_dim(live_slots, block_index, 0, keepdims=False)
        mask_words = lax.dynamic_index_in_dim(edge_bits, block_index, 0, keepdims=False)
        key_rows = jnp.stack([lax.dynamic_slice_in_dim(features, (block_ids[slot_pos] * block_rows).astype(jnp.int32), block_rows, 0) for slot_pos in range(slot_count)])
        value_rows = key_rows.reshape(slot_count, block_rows, head_count, head_width)
        target_query = jnp.einsum("qhc,hc->hq", query_values, attend_target, precision=precise)
        source_keys = jnp.einsum("skhc,hc->hsk", value_rows, attend_source, precision=precise)
        logit_sum = target_query[:, None, None, :] + source_keys[:, :, :, None]
        leaky_score = jnp.where(logit_sum > 0, logit_sum, 0.2 * logit_sum)
        bit_values = jnp.bitwise_and(jnp.right_shift(mask_words[:, :, None, :], bit_shift[None, None, :, None]), 1)
        allowed = bit_values.reshape(slot_count, block_rows, block_rows) > 0
        self_slot = (block_ids == block_index)[:, None, None]
        allowed = jnp.logical_or(allowed, jnp.logical_and(self_slot, diagonal[None]))
        allowed = jnp.logical_and(allowed, (slot_range < live_count)[:, None, None])
        masked = jnp.where(allowed[None], leaky_score, -jnp.inf)
        row_peak = jnp.max(masked, axis=(1, 2))
        weights = jnp.where(allowed[None], jnp.exp(leaky_score - row_peak[:, None, None, :]), 0.0)
        row_norm = jnp.sum(weights, axis=(1, 2))
        alpha = weights / row_norm[:, None, None, :]
        agg = jnp.einsum("hskq,skhc->qhc", alpha, value_rows, precision=precise)
        layer_block = jax.nn.elu(agg).reshape(block_rows, model_width)
        cot_rows = lax.dynamic_slice_in_dim(cotangent, row_start, block_rows, 0).reshape(block_rows, head_count, head_width)
        grad_agg = cot_rows * jnp.where(agg > 0, 1.0, jnp.exp(agg))
        row_delta = jnp.einsum("qhc,qhc->hq", grad_agg, agg, precision=precise)
        prob_grad = jnp.einsum("qhc,skhc->hskq", grad_agg, value_rows, precision=precise)
        score_grad = alpha * (prob_grad - row_delta[:, None, None, :]) * jnp.where(logit_sum > 0, 1.0, 0.2)
        target_part = jnp.sum(score_grad, axis=(1, 2))
        source_part = jnp.sum(score_grad, axis=3)
        value_grad = jnp.einsum("hskq,qhc->skhc", alpha, grad_agg, precision=precise)
        key_grad = value_grad + jnp.transpose(source_part, (1, 2, 0))[:, :, :, None] * attend_source[None, None]
        key_grad = key_grad.reshape(slot_count, block_rows, model_width)
        for slot_pos in range(slot_count):
            feature_grad = add_rows(feature_grad, key_grad[slot_pos], (block_ids[slot_pos] * block_rows).astype(jnp.int32))
        own_term = (target_part.T[:, :, None] * attend_target[None]).reshape(block_rows, model_width)
        feature_grad = add_rows(feature_grad, own_term, row_start)
        source_att = source_att + jnp.einsum("hsk,skhc->hc", source_part, value_rows, precision=precise)
        target_att = target_att + jnp.einsum("hq,qhc->hc", target_part, query_values, precision=precise)
        return (feature_grad, source_att, target_att), layer_block

    start_state = (jnp.zeros((node_count, model_width), jnp.float32), jnp.zeros((head_count, head_width), jnp.float32), jnp.zeros((head_count, head_width), jnp.float32))
    final_state, layer_blocks = lax.scan(per_block, start_state, jnp.arange(block_count, dtype=jnp.int32))
    feature_grad, source_att, target_att = final_state
    return layer_blocks.reshape(node_count, model_width), feature_grad, source_att, target_att
```

```python
import functools

import jax
import jax.numpy as jnp
from jax import lax
from jax.experimental import pallas as pl
from jax.experimental.pallas import tpu as pltpu
from jax.sharding import PartitionSpec as P

precise = lax.Precision.HIGHEST
MESH = pl.DeviceIdType.MESH
f32 = jnp.float32
bf16 = jnp.bfloat16


def split(value):
    high = value.astype(bf16)
    return high, (value - high.astype(f32)).astype(bf16)


def mm(left, right):
    return jnp.dot(left, right, preferred_element_type=f32)


def kernel(
    cycle,
    copies,
    feat_ref,
    source_ref,
    target_ref,
    blocks_ref,
    live_ref,
    edges_ref,
    cot_ref,
    out_ref,
    grad_ref,
    sgrad_ref,
    tgrad_ref,
    feats,
    srcs,
    bits,
    w_hi,
    w_lo,
    w_slope,
    agg,
    probs_a,
    probs_b,
    vals_hi,
    vals_lo,
    delta_s,
    sent,
    got,
    dst_sum,
    src_att,
    red,
    red2,
    feat_send,
    feat_recv,
    src_send,
    src_recv,
    grad_send,
    grad_recv,
    red_send,
    red_recv,
    red2_send,
    red2_recv,
):
    rows, width = feat_ref.shape
    heads, head = source_ref.shape
    slots = edges_ref.shape[0]
    count = 3 * copies
    pairs = heads // 2
    blk = lax.axis_index("blk")
    cp = lax.axis_index("copy")

    def place(c):
        group, turn = c // copies, c % copies
        shift = (group + 1) % 3 - 1
        return lax.rem(blk + shift + cycle, cycle), lax.rem(cp + turn, copies)

    def mirror(c):
        group, turn = c // copies, c % copies
        return (3 - group) % 3 * copies + (copies - turn) % copies

    barrier = pltpu.get_barrier_semaphore()
    for c in range(1, count):
        pl.semaphore_signal(barrier, inc=1, device_id=place(c), device_id_type=MESH)

    def greet(step, carry):
        pl.semaphore_signal(
            barrier, inc=1, device_id=(lax.rem(blk + step, cycle), cp), device_id_type=MESH
        )
        return carry

    lax.fori_loop(2, cycle - 1, greet, 0)

    lane = lax.broadcasted_iota(jnp.int32, (heads, width), 1)
    head_row = lax.broadcasted_iota(jnp.int32, (heads, width), 0)
    on_head = lane // head == head_row
    wide_source = jnp.where(on_head, jnp.concatenate([source_ref[...]] * heads, 1), 0.0)
    wide_target = jnp.where(on_head, jnp.concatenate([target_ref[...]] * heads, 1), 0.0)
    logits = lax.dot_general(
        jnp.concatenate([wide_source, wide_target], 0),
        feat_ref[...],
        (((1,), (1,)), ((), ())),
        precision=precise,
        preferred_element_type=f32,
    )
    srcs[0] = logits[:heads]
    dst = logits[heads:]

    pl.semaphore_wait(barrier, count - 1 + cycle - 3)

    def src_copy(c):
        return pltpu.make_async_remote_copy(
            src_ref=srcs.at[0],
            dst_ref=srcs.at[mirror(c)],
            send_sem=src_send.at[c],
            recv_sem=src_recv.at[mirror(c)],
            device_id=place(c),
            device_id_type=MESH,
        )

    def feat_copy(c):
        return pltpu.make_async_remote_copy(
            src_ref=feat_ref,
            dst_ref=feats.at[mirror(c)],
            send_sem=feat_send.at[c],
            recv_sem=feat_recv.at[mirror(c)],
            device_id=place(c),
            device_id_type=MESH,
        )

    def grad_copy(c):
        return pltpu.make_async_remote_copy(
            src_ref=sent.at[c],
            dst_ref=got.at[mirror(c)],
            send_sem=grad_send.at[c],
            recv_sem=grad_recv.at[mirror(c)],
            device_id=place(c),
            device_id_type=MESH,
        )

    for c in range(1, count):
        src_copy(c).start()
    for c in range(1, count):
        feat_copy(c).start()
    feats[0] = feat_ref[...]

    live = live_ref[0]
    for c in range(count):
        there, turn = place(c)
        block = there * copies + turn
        words = jnp.zeros(bits.shape[1:], jnp.int32)
        for slot in range(slots):
            chosen = jnp.logical_and(blocks_ref[0, slot] == block, slot < live)
            words = words + edges_ref[slot] * jnp.where(chosen, 1, 0)
        bits[c] = words

    cot_t = cot_ref[...].T
    bit = lax.broadcasted_iota(jnp.int32, (rows // 8, 8, rows), 1)
    key_row = lax.broadcasted_iota(jnp.int32, (rows, rows), 0)
    query_lane = lax.broadcasted_iota(jnp.int32, (rows, rows), 1)

    def mask_of(c):
        words = jnp.broadcast_to(bits[c][:, None, :], (rows // 8, 8, rows))
        mask = jnp.bitwise_and(jnp.right_shift(words, bit), 1).reshape(rows, rows)
        self_edge = jnp.where(key_row == query_lane, jnp.where(c == 0, 1, 0), 0)
        return jnp.bitwise_or(mask, self_edge) > 0

    for c in range(1, count):
        src_copy(mirror(c)).wait_recv()

    def peak_step(c, peaks):
        mask = mask_of(c)
        columns = srcs[c].T
        found = []
        for h in range(heads):
            masked = jnp.where(mask, columns[:, h : h + 1], -jnp.inf)
            found.append(jnp.maximum(peaks[h], jnp.max(masked, axis=0, keepdims=True)))
        return tuple(found)

    start = tuple(jnp.full((1, rows), -jnp.inf, f32) for _ in range(heads))
    tops = lax.fori_loop(0, count, peak_step, start)
    dsts = [dst[h : h + 1] for h in range(heads)]
    peaks = []
    for h in range(heads):
        top = dsts[h] + tops[h]
        peaks.append(jnp.where(top > 0, top, 0.2 * top))

    def weight_step(c, norms):
        mask = mask_of(c)
        columns = srcs[c].T
        sums = []
        for h in range(heads):
            logit = dsts[h] + columns[:, h : h + 1]
            up = logit > 0
            score = jnp.where(up, logit, 0.2 * logit)
            weight = jnp.where(mask, jnp.exp(score - peaks[h]), 0.0)
            sums.append(norms[h] + jnp.sum(weight, axis=0, keepdims=True))
            high, low = split(weight)
            w_hi[c, h] = high
            w_lo[c, h] = low
            w_slope[c, h] = jnp.where(up, weight, 0.2 * weight)
        return tuple(sums)

    zero_row = jnp.zeros((1, rows), f32)
    norms = lax.fori_loop(0, count, weight_step, (zero_row,) * heads)

    agg[...] = jnp.zeros(agg.shape, f32)

    def forward_step(c, carry):
        @pl.when(c > 0)
        def _():
            feat_copy(mirror(c)).wait_recv()

        high, low = split(feats[c].T)
        both = jnp.concatenate([high, low], 1)
        for h in range(heads):
            part = pl.ds(h * head, head)
            w_h = w_hi[c, h]
            agg[part, :] += mm(both[h * head : (h + 1) * head], jnp.concatenate([w_h, w_h], 0)) + mm(
                high[h * head : (h + 1) * head], w_lo[c, h]
            )
        return carry

    lax.fori_loop(0, count, forward_step, 0)

    flat_source = jnp.sum(wide_source, axis=0, keepdims=True)
    left = lax.broadcasted_iota(jnp.int32, (rows, rows), 1) < head
    zero_half = jnp.zeros((head, rows), f32)
    zero_tile = jnp.zeros((rows, rows), f32)
    ones_tile = jnp.ones((rows, rows), f32)
    for p in range(pairs):
        scaled, outs = [], []
        for h in (2 * p, 2 * p + 1):
            inverse = 1.0 / norms[h]
            agg_t = agg[h * head : (h + 1) * head, :] * inverse
            raised = jnp.exp(jnp.minimum(agg_t, 0.0))
            outs.append(jnp.where(agg_t > 0, agg_t, raised - 1.0))
            g_t = cot_t[h * head : (h + 1) * head] * jnp.where(agg_t > 0, 1.0, raised)
            delta_s[h] = jnp.sum(g_t * agg_t, axis=0, keepdims=True) * inverse
            scaled.append(g_t * inverse)
        out_ref[:, p * 2 * head : (p + 1) * 2 * head] = jnp.concatenate(outs, 0).T
        g_pair = jnp.concatenate(scaled, 0).T
        block = jnp.concatenate(
            [
                jnp.concatenate([scaled[0], zero_half], 1),
                jnp.concatenate([zero_half, scaled[1]], 1),
            ],
            0,
        )
        high, low = split(block)
        probs_a[p] = jnp.concatenate([high, high], 0)
        probs_b[p] = low
        a_pair = jnp.broadcast_to(flat_source[:, p * 2 * head : (p + 1) * 2 * head], (rows, rows))
        mixed = jnp.concatenate(
            [
                jnp.concatenate([jnp.where(left, g_pair, 0.0), zero_tile], 1),
                jnp.concatenate(
                    [jnp.where(left, a_pair, 0.0), jnp.where(left, ones_tile, 0.0)], 1
                ),
                jnp.concatenate([jnp.where(left, 0.0, g_pair), zero_tile], 1),
                jnp.concatenate(
                    [jnp.where(left, 0.0, a_pair), jnp.where(left, 0.0, ones_tile)], 1
                ),
            ],
            0,
        )
        high, low = split(mixed)
        vals_hi[p] = high
        vals_lo[p] = low

    dst_sum[...] = jnp.zeros(dst_sum.shape, f32)
    src_att[...] = jnp.zeros(src_att.shape, f32)

    def backward_step(step, carry):
        c = lax.rem(step + 1, count)
        for p in range(pairs):
            tile = pl.ds(p * 2 * head, 2 * head)
            value = feats[c, :, tile]
            high, low = split(value)
            prob = mm(jnp.concatenate([high, low], 1), probs_a[p]) + mm(high, probs_b[p])
            highs, lows = [], []
            for side in range(2):
                h = 2 * p + side
                score = w_slope[c, h] * (prob[:, side * rows : (side + 1) * rows] - delta_s[h])
                dst_sum[h] += jnp.sum(score, axis=0, keepdims=True)
                s_hi, s_lo = split(score)
                highs += [w_hi[c, h], s_hi]
                lows += [w_lo[c, h], s_lo]
            left_hi = jnp.concatenate(highs, 1)
            left_lo = jnp.concatenate(lows, 1)
            both = mm(left_hi, vals_hi[p]) + mm(left_lo, vals_hi[p]) + mm(left_hi, vals_lo[p])
            sent[c, :, tile] = both[:, : 2 * head]
            src_att[p] += jnp.sum(both[:, 2 * head :] * value, axis=0, keepdims=True)

        @pl.when(c > 0)
        def _():
            grad_copy(c).start()

        return carry

    lax.fori_loop(0, count, backward_step, 0)

    dst_rows = jnp.concatenate([dst_sum[h] for h in range(heads)], 0)
    tgt_att = jnp.dot(dst_rows, feat_ref[...], precision=precise, preferred_element_type=f32)
    tgt_att = jnp.sum(jnp.where(on_head, tgt_att, 0.0), axis=0, keepdims=True)
    for p in range(pairs):
        red[blk, p : p + 1, :] = src_att[p]
        red[blk, pairs + p : pairs + p + 1, :] = tgt_att[:, p * 2 * head : (p + 1) * 2 * head]

    def red_copy(step, here):
        return pltpu.make_async_remote_copy(
            src_ref=red.at[here],
            dst_ref=red.at[here],
            send_sem=red_send.at[step],
            recv_sem=red_recv.at[here],
            device_id=(lax.rem(blk + step, cycle), cp),
            device_id_type=MESH,
        )

    def red_start(step, carry):
        red_copy(step, blk).start()
        return carry

    lax.fori_loop(1, cycle, red_start, 0)

    own_term = jnp.dot(dst_rows.T, wide_target, precision=precise, preferred_element_type=f32)
    grad_ref[...] = sent[0] + own_term

    def red_wait(step, carry):
        red_copy(step, lax.rem(blk + step, cycle)).wait_recv()
        return carry

    lax.fori_loop(1, cycle, red_wait, 0)
    total = red[0]
    for i in range(1, cycle):
        total = total + red[i]
    red2[cp] = total

    def red2_copy(turn, here):
        return pltpu.make_async_remote_copy(
            src_ref=red2.at[here],
            dst_ref=red2.at[here],
            send_sem=red2_send.at[turn],
            recv_sem=red2_recv.at[here],
            device_id=(blk, lax.rem(cp + turn, copies)),
            device_id_type=MESH,
        )

    for turn in range(1, copies):
        red2_copy(turn, cp).start()

    def grad_step(c, carry):
        grad_copy(mirror(c)).wait_recv()
        grad_ref[...] += got[c]
        return carry

    lax.fori_loop(1, count, grad_step, 0)

    for turn in range(1, copies):
        red2_copy(turn, lax.rem(cp + turn, copies)).wait_recv()
    total = red2[0]
    for i in range(1, copies):
        total = total + red2[i]
    for p in range(pairs):
        for side in range(2):
            h = 2 * p + side
            span = slice(side * head, (side + 1) * head)
            sgrad_ref[h : h + 1, :] = total[p : p + 1, span]
            tgrad_ref[h : h + 1, :] = total[pairs + p : pairs + p + 1, span]

    for c in range(1, count):
        src_copy(c).wait_send()
        feat_copy(c).wait_send()
        grad_copy(c).wait_send()

    def red_sent(step, carry):
        red_copy(step, blk).wait_send()
        return carry

    lax.fori_loop(1, cycle, red_sent, 0)
    for turn in range(1, copies):
        red2_copy(turn, cp).wait_send()


def per_device(
    features, attend_source, attend_target, key_blocks, live_slots, edge_bits, cotangent
):
    heads, head = attend_source.shape
    rows, width = features.shape
    copies = lax.axis_size("copy")
    cycle = lax.axis_size("blk")
    count = 3 * copies
    pairs = heads // 2
    slots, word_rows = edge_bits.shape[1:3]
    vmem = pl.BlockSpec(memory_space=pltpu.VMEM)
    smem = pl.BlockSpec(memory_space=pltpu.SMEM)
    dma = pltpu.SemaphoreType.DMA
    return pl.pallas_call(
        functools.partial(kernel, cycle, copies),
        out_shape=(
            jax.ShapeDtypeStruct((rows, width), f32),
            jax.ShapeDtypeStruct((rows, width), f32),
            jax.ShapeDtypeStruct((heads, head), f32),
            jax.ShapeDtypeStruct((heads, head), f32),
        ),
        in_specs=[vmem, vmem, vmem, smem, smem, vmem, vmem],
        out_specs=(vmem,) * 4,
        scratch_shapes=[
            pltpu.VMEM((count, rows, width), f32),
            pltpu.VMEM((count, heads, rows), f32),
            pltpu.VMEM((count, word_rows, rows), jnp.int32),
            pltpu.VMEM((count, heads, rows, rows), bf16),
            pltpu.VMEM((count, heads, rows, rows), bf16),
            pltpu.VMEM((count, heads, rows, rows), f32),
            pltpu.VMEM((width, rows), f32),
            pltpu.VMEM((pairs, 2 * rows, 2 * rows), bf16),
            pltpu.VMEM((pairs, rows, 2 * rows), bf16),
            pltpu.VMEM((pairs, 4 * rows, 2 * rows), bf16),
            pltpu.VMEM((pairs, 4 * rows, 2 * rows), bf16),
            pltpu.VMEM((heads, 1, rows), f32),
            pltpu.VMEM((count, rows, width), f32),
            pltpu.VMEM((count, rows, width), f32),
            pltpu.VMEM((heads, 1, rows), f32),
            pltpu.VMEM((pairs, 1, 2 * head), f32),
            pltpu.VMEM((cycle, heads, 2 * head), f32),
            pltpu.VMEM((copies, heads, 2 * head), f32),
            dma((count,)),
            dma((count,)),
            dma((count,)),
            dma((count,)),
            dma((count,)),
            dma((count,)),
            dma((cycle,)),
            dma((cycle,)),
            dma((copies,)),
            dma((copies,)),
        ],
        compiler_params=pltpu.CompilerParams(
            collective_id=0, has_side_effects=True, vmem_limit_bytes=52 * 1024 * 1024
        ),
    )(
        features,
        attend_source,
        attend_target,
        key_blocks,
        live_slots,
        edge_bits.reshape(slots, word_rows, rows),
        cotangent,
    )


def solution(mesh):
    placed = (
        P(("blk", "copy"), None),
        P(),
        P(),
        P(("blk", "copy"), None),
        P(("blk", "copy")),
        P(("blk", "copy"), None, None, None),
        P(("blk", "copy"), None),
    )
    return jax.shard_map(
        per_device,
        mesh=mesh,
        in_specs=placed,
        out_specs=(P(("blk", "copy"), None), P(("blk", "copy"), None), P(), P()),
        check_vma=False,
    )
```

```python
import functools

import jax
import jax.numpy as jnp
from jax import lax
from jax.experimental import pallas as pl
from jax.experimental.pallas import tpu as pltpu
from jax.sharding import PartitionSpec as P

precise = lax.Precision.HIGHEST
MESH = pl.DeviceIdType.MESH
f32 = jnp.float32
bf16 = jnp.bfloat16


def split(value):
    high = value.astype(bf16)
    return high, (value - high.astype(f32)).astype(bf16)


def mm(left, right):
    return jnp.dot(left, right, preferred_element_type=f32)


def kernel(
    cycle,
    copies,
    feat_hbm,
    source_hbm,
    target_hbm,
    blocks_hbm,
    live_hbm,
    edges_hbm,
    cot_hbm,
    out_ref,
    grad_ref,
    sgrad_ref,
    tgrad_ref,
    source_ref,
    target_ref,
    blocks_ref,
    live_ref,
    edges_ref,
    cot_ref,
    feats,
    srcs,
    bits,
    w_hi,
    w_lo,
    w_slope,
    agg,
    probs_a,
    probs_b,
    vals_hi,
    vals_lo,
    delta_s,
    sent,
    got,
    dst_sum,
    src_att,
    red,
    red2,
    feat_send,
    feat_recv,
    src_send,
    src_recv,
    grad_send,
    grad_recv,
    red_send,
    red_recv,
    red2_send,
    red2_recv,
    local_sem,
    low_recv,
    near_send,
    far_send,
    low_send,
):
    rows, width = feat_hbm.shape
    half = rows // 2
    feat_ref = feats.at[0]
    heads, head = source_ref.shape
    slots = edges_ref.shape[0]
    count = 3 * copies
    pairs = heads // 2
    blk = lax.axis_index("blk")
    cp = lax.axis_index("copy")

    def place(c):
        group, turn = c // copies, c % copies
        shift = ((group + 1) % 3 - 1) * (1 - 2 * lax.rem(blk, 2))
        return lax.rem(blk + shift + cycle, cycle), lax.rem(cp + turn, copies)

    def mirror(c):
        group, turn = c // copies, c % copies
        return group * copies + (copies - turn) % copies

    loads = [
        pltpu.make_async_copy(source, target, local_sem.at[i])
        for i, (source, target) in enumerate(
            (
                (feat_hbm, feat_ref),
                (source_hbm, source_ref),
                (target_hbm, target_ref),
                (blocks_hbm, blocks_ref),
                (live_hbm, live_ref),
                (edges_hbm, edges_ref),
                (cot_hbm, cot_ref),
            )
        )
    ]
    for load in loads:
        load.start()

    barrier = pltpu.get_barrier_semaphore()
    for c in range(1, count):
        pl.semaphore_signal(barrier, inc=1, device_id=place(c), device_id_type=MESH)

    def greet(step, carry):
        pl.semaphore_signal(
            barrier, inc=1, device_id=(lax.rem(blk + step, cycle), cp), device_id_type=MESH
        )
        return carry

    lax.fori_loop(2, cycle - 1, greet, 0)

    for load in loads[:3]:
        load.wait()
    lane = lax.broadcasted_iota(jnp.int32, (heads, width), 1)
    head_row = lax.broadcasted_iota(jnp.int32, (heads, width), 0)
    on_head = lane // head == head_row
    wide_source = jnp.where(on_head, jnp.concatenate([source_ref[...]] * heads, 1), 0.0)
    wide_target = jnp.where(on_head, jnp.concatenate([target_ref[...]] * heads, 1), 0.0)
    logits = lax.dot_general(
        jnp.concatenate([wide_source, wide_target], 0),
        feat_ref[...],
        (((1,), (1,)), ((), ())),
        precision=precise,
        preferred_element_type=f32,
    )
    srcs[0] = logits[:heads]
    dst = logits[heads:]

    pl.semaphore_wait(barrier, count - 1 + cycle - 3)

    def src_copy(c):
        return pltpu.make_async_remote_copy(
            src_ref=srcs.at[0],
            dst_ref=srcs.at[mirror(c)],
            send_sem=src_send.at[c],
            recv_sem=src_recv.at[mirror(c)],
            device_id=place(c),
            device_id_type=MESH,
        )

    def feat_copy(c):
        return pltpu.make_async_remote_copy(
            src_ref=feat_hbm,
            dst_ref=feats.at[mirror(c)],
            send_sem=feat_send.at[c],
            recv_sem=feat_recv.at[mirror(c)],
            device_id=place(c),
            device_id_type=MESH,
        )

    def near_copy(turn):
        return pltpu.make_async_remote_copy(
            src_ref=feats.at[turn],
            dst_ref=feats.at[copies + turn],
            send_sem=near_send.at[turn],
            recv_sem=feat_recv.at[copies + turn],
            device_id=place(copies),
            device_id_type=MESH,
        )

    def far_copy(turn):
        return pltpu.make_async_remote_copy(
            src_ref=feats.at[turn, pl.ds(0, half)],
            dst_ref=feats.at[2 * copies + turn, pl.ds(0, half)],
            send_sem=far_send.at[turn],
            recv_sem=feat_recv.at[2 * copies + turn],
            device_id=place(2 * copies),
            device_id_type=MESH,
        )

    def low_copy(turn):
        return pltpu.make_async_remote_copy(
            src_ref=feats.at[2 * copies, pl.ds(half, half)],
            dst_ref=feats.at[mirror(2 * copies + turn), pl.ds(half, half)],
            send_sem=low_send.at[turn],
            recv_sem=low_recv.at[mirror(turn)],
            device_id=place(turn),
            device_id_type=MESH,
        )

    def grad_copy(c):
        return pltpu.make_async_remote_copy(
            src_ref=sent.at[c],
            dst_ref=got.at[mirror(c)],
            send_sem=grad_send.at[c],
            recv_sem=grad_recv.at[mirror(c)],
            device_id=place(c),
            device_id_type=MESH,
        )

    for c in range(1, count):
        src_copy(c).start()
    direct = list(range(1, copies)) + [2 * copies, copies]
    for c in direct:
        feat_copy(c).start()
    for load in loads[3:]:
        load.wait()

    live = live_ref[...]
    for c in range(count):
        there, turn = place(c)
        block = there * copies + turn
        words = jnp.zeros(bits.shape[1:], jnp.int32)
        for slot in range(slots):
            chosen = jnp.logical_and(blocks_ref[:, slot : slot + 1] == block, slot < live)
            words = words + edges_ref[slot] * jnp.where(chosen, 1, 0)
        bits[c] = words

    cot_t = cot_ref[...].T
    bit = lax.broadcasted_iota(jnp.int32, (rows // 8, 8, rows), 1)
    key_row = lax.broadcasted_iota(jnp.int32, (rows, rows), 0)
    query_lane = lax.broadcasted_iota(jnp.int32, (rows, rows), 1)

    def mask_of(c):
        words = jnp.broadcast_to(bits[c][:, None, :], (rows // 8, 8, rows))
        mask = jnp.bitwise_and(jnp.right_shift(words, bit), 1).reshape(rows, rows)
        self_edge = jnp.where(key_row == query_lane, jnp.where(c == 0, 1, 0), 0)
        return jnp.bitwise_or(mask, self_edge) > 0

    for c in range(1, count):
        src_copy(mirror(c)).wait_recv()

    def peak_step(c, peaks):
        mask = mask_of(c)
        columns = srcs[c].T
        found = []
        for h in range(heads):
            masked = jnp.where(mask, columns[:, h : h + 1], -jnp.inf)
            found.append(jnp.maximum(peaks[h], jnp.max(masked, axis=0, keepdims=True)))
        return tuple(found)

    start = tuple(jnp.full((1, rows), -jnp.inf, f32) for _ in range(heads))
    tops = lax.fori_loop(0, count, peak_step, start)
    dsts = [dst[h : h + 1] for h in range(heads)]
    peaks = []
    for h in range(heads):
        top = dsts[h] + tops[h]
        peaks.append(jnp.where(top > 0, top, 0.2 * top))

    def weight_step(c, norms):
        mask = mask_of(c)
        columns = srcs[c].T
        sums = []
        for h in range(heads):
            logit = dsts[h] + columns[:, h : h + 1]
            up = logit > 0
            score = jnp.where(up, logit, 0.2 * logit)
            weight = jnp.where(mask, jnp.exp(score - peaks[h]), 0.0)
            sums.append(norms[h] + jnp.sum(weight, axis=0, keepdims=True))
            high, low = split(weight)
            w_hi[c, h] = high
            w_lo[c, h] = low
            w_slope[c, h] = jnp.where(up, weight, 0.2 * weight)
        return tuple(sums)

    zero_row = jnp.zeros((1, rows), f32)
    norms = lax.fori_loop(0, copies + 1, weight_step, (zero_row,) * heads)
    for turn in range(1, copies):
        feat_copy(mirror(turn)).wait_recv()
        far_copy(turn).start()
        near_copy(turn).start()
    feat_copy(2 * copies).wait_recv()
    for turn in range(1, copies):
        low_copy(turn).start()
    norms = lax.fori_loop(copies + 1, count, weight_step, norms)

    agg[...] = jnp.zeros(agg.shape, f32)

    def forward_step(c, carry):
        @pl.when(c == copies)
        def _():
            feat_copy(copies).wait_recv()

        @pl.when(jnp.logical_and(c > copies, c < 2 * copies))
        def _():
            near_copy(c - copies).wait_recv()

        @pl.when(c > 2 * copies)
        def _():
            far_copy(c - 2 * copies).wait_recv()
            low_copy(mirror(c - 2 * copies)).wait_recv()

        high, low = split(feats[c].T)
        both = jnp.concatenate([high, low], 1)
        for h in range(heads):
            part = pl.ds(h * head, head)
            w_h = w_hi[c, h]
            agg[part, :] += mm(both[h * head : (h + 1) * head], jnp.concatenate([w_h, w_h], 0)) + mm(
                high[h * head : (h + 1) * head], w_lo[c, h]
            )
        return carry

    lax.fori_loop(0, count, forward_step, 0)

    flat_source = jnp.sum(wide_source, axis=0, keepdims=True)
    left = lax.broadcasted_iota(jnp.int32, (rows, rows), 1) < head
    zero_half = jnp.zeros((head, rows), f32)
    zero_tile = jnp.zeros((rows, rows), f32)
    ones_tile = jnp.ones((rows, rows), f32)
    for p in range(pairs):
        scaled, outs = [], []
        for h in (2 * p, 2 * p + 1):
            inverse = 1.0 / norms[h]
            agg_t = agg[h * head : (h + 1) * head, :] * inverse
            raised = jnp.exp(jnp.minimum(agg_t, 0.0))
            outs.append(jnp.where(agg_t > 0, agg_t, raised - 1.0))
            g_t = cot_t[h * head : (h + 1) * head] * jnp.where(agg_t > 0, 1.0, raised)
            delta_s[h] = jnp.sum(g_t * agg_t, axis=0, keepdims=True) * inverse
            scaled.append(g_t * inverse)
        out_ref[:, p * 2 * head : (p + 1) * 2 * head] = jnp.concatenate(outs, 0).T
        g_pair = jnp.concatenate(scaled, 0).T
        block = jnp.concatenate(
            [
                jnp.concatenate([scaled[0], zero_half], 1),
                jnp.concatenate([zero_half, scaled[1]], 1),
            ],
            0,
        )
        high, low = split(block)
        probs_a[p] = jnp.concatenate([high, high], 0)
        probs_b[p] = low
        a_pair = jnp.broadcast_to(flat_source[:, p * 2 * head : (p + 1) * 2 * head], (rows, rows))
        mixed = jnp.concatenate(
            [
                jnp.concatenate([jnp.where(left, g_pair, 0.0), zero_tile], 1),
                jnp.concatenate(
                    [jnp.where(left, a_pair, 0.0), jnp.where(left, ones_tile, 0.0)], 1
                ),
                jnp.concatenate([jnp.where(left, 0.0, g_pair), zero_tile], 1),
                jnp.concatenate(
                    [jnp.where(left, 0.0, a_pair), jnp.where(left, 0.0, ones_tile)], 1
                ),
            ],
            0,
        )
        high, low = split(mixed)
        vals_hi[p] = high
        vals_lo[p] = low

    dst_sum[...] = jnp.zeros(dst_sum.shape, f32)
    src_att[...] = jnp.zeros(src_att.shape, f32)

    def backward_step(step, carry):
        c = lax.rem(step + 1, count)
        for p in range(pairs):
            tile = pl.ds(p * 2 * head, 2 * head)
            value = feats[c, :, tile]
            high, low = split(value)
            prob = mm(jnp.concatenate([high, low], 1), probs_a[p]) + mm(high, probs_b[p])
            highs, lows = [], []
            for side in range(2):
                h = 2 * p + side
                score = w_slope[c, h] * (prob[:, side * rows : (side + 1) * rows] - delta_s[h])
                dst_sum[h] += jnp.sum(score, axis=0, keepdims=True)
                s_hi, s_lo = split(score)
                highs += [w_hi[c, h], s_hi]
                lows += [w_lo[c, h], s_lo]
            left_hi = jnp.concatenate(highs, 1)
            left_lo = jnp.concatenate(lows, 1)
            both = mm(left_hi, vals_hi[p]) + mm(left_lo, vals_hi[p]) + mm(left_hi, vals_lo[p])
            sent[c, :, tile] = both[:, : 2 * head]
            src_att[p] += jnp.sum(both[:, 2 * head :] * value, axis=0, keepdims=True)

        @pl.when(c > 0)
        def _():
            grad_copy(c).start()

        return carry

    lax.fori_loop(0, count, backward_step, 0)

    dst_rows = jnp.concatenate([dst_sum[h] for h in range(heads)], 0)
    tgt_att = jnp.dot(dst_rows, feat_ref[...], precision=precise, preferred_element_type=f32)
    tgt_att = jnp.sum(jnp.where(on_head, tgt_att, 0.0), axis=0, keepdims=True)
    for p in range(pairs):
        red[blk, p : p + 1, :] = src_att[p]
        red[blk, pairs + p : pairs + p + 1, :] = tgt_att[:, p * 2 * head : (p + 1) * 2 * head]

    def red_copy(step, here):
        return pltpu.make_async_remote_copy(
            src_ref=red.at[here],
            dst_ref=red.at[here],
            send_sem=red_send.at[step],
            recv_sem=red_recv.at[here],
            device_id=(lax.rem(blk + step, cycle), cp),
            device_id_type=MESH,
        )

    def red_start(step, carry):
        red_copy(step, blk).start()
        return carry

    lax.fori_loop(1, cycle, red_start, 0)

    own_term = jnp.dot(dst_rows.T, wide_target, precision=precise, preferred_element_type=f32)
    grad_ref[...] = sent[0] + own_term

    def red_wait(step, carry):
        red_copy(step, lax.rem(blk + step, cycle)).wait_recv()
        return carry

    lax.fori_loop(1, cycle, red_wait, 0)
    total = red[0]
    for i in range(1, cycle):
        total = total + red[i]
    red2[cp] = total

    def red2_copy(turn, here):
        return pltpu.make_async_remote_copy(
            src_ref=red2.at[here],
            dst_ref=red2.at[here],
            send_sem=red2_send.at[turn],
            recv_sem=red2_recv.at[here],
            device_id=(blk, lax.rem(cp + turn, copies)),
            device_id_type=MESH,
        )

    for turn in range(1, copies):
        red2_copy(turn, cp).start()

    def grad_step(c, carry):
        grad_copy(mirror(c)).wait_recv()
        grad_ref[...] += got[c]
        return carry

    lax.fori_loop(1, count, grad_step, 0)

    for turn in range(1, copies):
        red2_copy(turn, lax.rem(cp + turn, copies)).wait_recv()
    total = red2[0]
    for i in range(1, copies):
        total = total + red2[i]
    for p in range(pairs):
        for side in range(2):
            h = 2 * p + side
            span = slice(side * head, (side + 1) * head)
            sgrad_ref[h : h + 1, :] = total[p : p + 1, span]
            tgrad_ref[h : h + 1, :] = total[pairs + p : pairs + p + 1, span]

    for c in range(1, count):
        src_copy(c).wait_send()
        grad_copy(c).wait_send()
    for c in direct:
        feat_copy(c).wait_send()
    for turn in range(1, copies):
        near_copy(turn).wait_send()
        far_copy(turn).wait_send()
        low_copy(turn).wait_send()

    def red_sent(step, carry):
        red_copy(step, blk).wait_send()
        return carry

    lax.fori_loop(1, cycle, red_sent, 0)
    for turn in range(1, copies):
        red2_copy(turn, cp).wait_send()


def settle(*refs):
    sems = refs[-1]
    count = len(refs) // 2
    moves = [
        pltpu.make_async_copy(refs[i], refs[count + i], sems.at[i]) for i in range(count)
    ]
    for move in moves:
        move.start()
    for move in moves:
        move.wait()


def per_device(
    features, attend_source, attend_target, key_blocks, live_slots, edge_bits, cotangent
):
    heads, head = attend_source.shape
    rows, width = features.shape
    copies = lax.axis_size("copy")
    cycle = lax.axis_size("blk")
    count = 3 * copies
    pairs = heads // 2
    slots, word_rows = edge_bits.shape[1:3]
    vmem = pl.BlockSpec(memory_space=pltpu.VMEM)
    hbm = pl.BlockSpec(memory_space=pltpu.HBM)
    anywhere = pl.BlockSpec(memory_space=pl.ANY)
    dma = pltpu.SemaphoreType.DMA
    shapes = (
        jax.ShapeDtypeStruct((rows, width), f32),
        jax.ShapeDtypeStruct((rows, width), f32),
        jax.ShapeDtypeStruct((heads, head), f32),
        jax.ShapeDtypeStruct((heads, head), f32),
    )
    found = pl.pallas_call(
        functools.partial(kernel, cycle, copies),
        out_shape=shapes,
        in_specs=[hbm] * 7,
        out_specs=(vmem,) * 4,
        scratch_shapes=[
            pltpu.VMEM((heads, head), f32),
            pltpu.VMEM((heads, head), f32),
            pltpu.VMEM((1, slots), jnp.int32),
            pltpu.VMEM((1, 1), jnp.int32),
            pltpu.VMEM((slots, word_rows, rows), jnp.int32),
            pltpu.VMEM((rows, width), f32),
            pltpu.VMEM((count, rows, width), f32),
            pltpu.VMEM((count, heads, rows), f32),
            pltpu.VMEM((count, word_rows, rows), jnp.int32),
            pltpu.VMEM((count, heads, rows, rows), bf16),
            pltpu.VMEM((count, heads, rows, rows), bf16),
            pltpu.VMEM((count, heads, rows, rows), f32),
            pltpu.VMEM((width, rows), f32),
            pltpu.VMEM((pairs, 2 * rows, 2 * rows), bf16),
            pltpu.VMEM((pairs, rows, 2 * rows), bf16),
            pltpu.VMEM((pairs, 4 * rows, 2 * rows), bf16),
            pltpu.VMEM((pairs, 4 * rows, 2 * rows), bf16),
            pltpu.VMEM((heads, 1, rows), f32),
            pltpu.VMEM((count, rows, width), f32),
            pltpu.VMEM((count, rows, width), f32),
            pltpu.VMEM((heads, 1, rows), f32),
            pltpu.VMEM((pairs, 1, 2 * head), f32),
            pltpu.VMEM((cycle, heads, 2 * head), f32),
            pltpu.VMEM((copies, heads, 2 * head), f32),
            dma((count,)),
            dma((count,)),
            dma((count,)),
            dma((count,)),
            dma((count,)),
            dma((count,)),
            dma((cycle,)),
            dma((cycle,)),
            dma((copies,)),
            dma((copies,)),
            dma((7,)),
            dma((copies,)),
            dma((copies,)),
            dma((copies,)),
            dma((copies,)),
        ],
        compiler_params=pltpu.CompilerParams(
            collective_id=0, has_side_effects=True, vmem_limit_bytes=63 * 1024 * 1024
        ),
    )(
        features,
        attend_source,
        attend_target,
        key_blocks,
        live_slots.reshape(1, 1),
        edge_bits.reshape(slots, word_rows, rows),
        cotangent,
    )
    return pl.pallas_call(
        settle,
        out_shape=shapes,
        in_specs=[anywhere] * 4,
        out_specs=(anywhere,) * 4,
        scratch_shapes=[dma((4,))],
        compiler_params=pltpu.CompilerParams(vmem_limit_bytes=63 * 1024 * 1024),
    )(*found)


def solution(mesh):
    placed = (
        P(("blk", "copy"), None),
        P(),
        P(),
        P(("blk", "copy"), None),
        P(("blk", "copy")),
        P(("blk", "copy"), None, None, None),
        P(("blk", "copy"), None),
    )
    return jax.shard_map(
        per_device,
        mesh=mesh,
        in_specs=placed,
        out_specs=(P(("blk", "copy"), None), P(("blk", "copy"), None), P(), P()),
        check_vma=False,
    )
```

```python
import functools

import jax
import jax.numpy as jnp
from jax import lax
from jax.experimental import pallas as pl
from jax.experimental.pallas import tpu as pltpu
from jax.sharding import PartitionSpec as P

precise = lax.Precision.HIGHEST
MESH = pl.DeviceIdType.MESH
f32 = jnp.float32
bf16 = jnp.bfloat16


def split(value):
    high = value.astype(bf16)
    return high, (value - high.astype(f32)).astype(bf16)


def mm(left, right):
    return jnp.dot(left, right, preferred_element_type=f32)


def kernel(
    cycle,
    copies,
    feat_hbm,
    source_hbm,
    target_hbm,
    blocks_hbm,
    live_hbm,
    edges_hbm,
    cot_hbm,
    out_ref,
    grad_ref,
    sgrad_ref,
    tgrad_ref,
    source_ref,
    target_ref,
    blocks_ref,
    live_ref,
    edges_ref,
    cot_ref,
    feats,
    srcs,
    bits,
    w_hi,
    w_lo,
    w_slope,
    agg,
    probs_a,
    probs_b,
    vals_hi,
    vals_lo,
    delta_s,
    sent,
    got,
    dst_sum,
    src_att,
    red,
    red2,
    feat_send,
    feat_recv,
    src_send,
    src_recv,
    grad_send,
    grad_recv,
    red_send,
    red_recv,
    red2_send,
    red2_recv,
    local_sem,
    low_recv,
    near_send,
    far_send,
    low_send,
):
    rows, width = feat_hbm.shape
    half = rows // 2
    feat_ref = feats.at[0]
    heads, head = source_ref.shape
    slots = edges_ref.shape[0]
    count = 3 * copies
    pairs = heads // 2
    blk = lax.axis_index("blk")
    cp = lax.axis_index("copy")

    def place(c):
        group, turn = c // copies, c % copies
        shift = ((group + 1) % 3 - 1) * (1 - 2 * lax.rem(blk, 2))
        return lax.rem(blk + shift + cycle, cycle), lax.rem(cp + turn, copies)

    def mirror(c):
        group, turn = c // copies, c % copies
        return group * copies + (copies - turn) % copies

    loads = [
        pltpu.make_async_copy(source, target, local_sem.at[i])
        for i, (source, target) in enumerate(
            (
                (feat_hbm, feat_ref),
                (source_hbm, source_ref),
                (target_hbm, target_ref),
                (blocks_hbm, blocks_ref),
                (live_hbm, live_ref),
                (edges_hbm, edges_ref),
                (cot_hbm, cot_ref),
            )
        )
    ]
    for load in loads:
        load.start()

    barrier = pltpu.get_barrier_semaphore()
    for c in range(1, count):
        pl.semaphore_signal(barrier, inc=1, device_id=place(c), device_id_type=MESH)

    def greet(step, carry):
        pl.semaphore_signal(
            barrier, inc=1, device_id=(lax.rem(blk + step, cycle), cp), device_id_type=MESH
        )
        return carry

    lax.fori_loop(2, cycle - 1, greet, 0)

    for load in loads[:3]:
        load.wait()
    lane = lax.broadcasted_iota(jnp.int32, (heads, width), 1)
    head_row = lax.broadcasted_iota(jnp.int32, (heads, width), 0)
    on_head = lane // head == head_row
    wide_source = jnp.where(on_head, jnp.concatenate([source_ref[...]] * heads, 1), 0.0)
    wide_target = jnp.where(on_head, jnp.concatenate([target_ref[...]] * heads, 1), 0.0)
    logits = lax.dot_general(
        jnp.concatenate([wide_source, wide_target], 0),
        feat_ref[...],
        (((1,), (1,)), ((), ())),
        precision=precise,
        preferred_element_type=f32,
    )
    srcs[0] = logits[:heads]
    dst = logits[heads:]

    pl.semaphore_wait(barrier, count - 1 + cycle - 3)

    def src_copy(c):
        return pltpu.make_async_remote_copy(
            src_ref=srcs.at[0],
            dst_ref=srcs.at[mirror(c)],
            send_sem=src_send.at[c],
            recv_sem=src_recv.at[mirror(c)],
            device_id=place(c),
            device_id_type=MESH,
        )

    def feat_copy(c):
        return pltpu.make_async_remote_copy(
            src_ref=feat_hbm,
            dst_ref=feats.at[mirror(c)],
            send_sem=feat_send.at[c],
            recv_sem=feat_recv.at[mirror(c)],
            device_id=place(c),
            device_id_type=MESH,
        )

    def near_copy(turn):
        return pltpu.make_async_remote_copy(
            src_ref=feats.at[turn],
            dst_ref=feats.at[copies + turn],
            send_sem=near_send.at[turn],
            recv_sem=feat_recv.at[copies + turn],
            device_id=place(copies),
            device_id_type=MESH,
        )

    def far_copy(turn):
        return pltpu.make_async_remote_copy(
            src_ref=feats.at[turn, pl.ds(0, half)],
            dst_ref=feats.at[2 * copies + turn, pl.ds(0, half)],
            send_sem=far_send.at[turn],
            recv_sem=feat_recv.at[2 * copies + turn],
            device_id=place(2 * copies),
            device_id_type=MESH,
        )

    def low_copy(turn):
        return pltpu.make_async_remote_copy(
            src_ref=feats.at[2 * copies, pl.ds(half, half)],
            dst_ref=feats.at[mirror(2 * copies + turn), pl.ds(half, half)],
            send_sem=low_send.at[turn],
            recv_sem=low_recv.at[mirror(turn)],
            device_id=place(turn),
            device_id_type=MESH,
        )

    def grad_copy(c):
        return pltpu.make_async_remote_copy(
            src_ref=sent.at[c],
            dst_ref=got.at[mirror(c)],
            send_sem=grad_send.at[c],
            recv_sem=grad_recv.at[mirror(c)],
            device_id=place(c),
            device_id_type=MESH,
        )

    for c in range(1, count):
        src_copy(c).start()
    direct = list(range(1, copies)) + [2 * copies, copies]
    for c in direct:
        feat_copy(c).start()
    for load in loads[3:]:
        load.wait()

    live = live_ref[...]
    for c in range(count):
        there, turn = place(c)
        block = there * copies + turn
        words = jnp.zeros(bits.shape[1:], jnp.int32)
        for slot in range(slots):
            chosen = jnp.logical_and(blocks_ref[:, slot : slot + 1] == block, slot < live)
            words = words + edges_ref[slot] * jnp.where(chosen, 1, 0)
        bits[c] = words

    cot_t = cot_ref[...].T
    bit = lax.broadcasted_iota(jnp.int32, (rows // 8, 8, rows), 1)
    key_row = lax.broadcasted_iota(jnp.int32, (rows, rows), 0)
    query_lane = lax.broadcasted_iota(jnp.int32, (rows, rows), 1)

    def mask_of(c):
        words = jnp.broadcast_to(bits[c][:, None, :], (rows // 8, 8, rows))
        mask = jnp.bitwise_and(jnp.right_shift(words, bit), 1).reshape(rows, rows)
        self_edge = jnp.where(key_row == query_lane, jnp.where(c == 0, 1, 0), 0)
        return jnp.bitwise_or(mask, self_edge) > 0

    for c in range(1, count):
        src_copy(mirror(c)).wait_recv()

    def peak_step(c, peaks):
        mask = mask_of(c)
        columns = srcs[c].T
        found = []
        for h in range(heads):
            masked = jnp.where(mask, columns[:, h : h + 1], -jnp.inf)
            found.append(jnp.maximum(peaks[h], jnp.max(masked, axis=0, keepdims=True)))
        return tuple(found)

    start = tuple(jnp.full((1, rows), -jnp.inf, f32) for _ in range(heads))
    tops = lax.fori_loop(0, count, peak_step, start)
    dsts = [dst[h : h + 1] for h in range(heads)]
    peaks = []
    for h in range(heads):
        top = dsts[h] + tops[h]
        peaks.append(jnp.where(top > 0, top, 0.2 * top))

    def weight_step(c, norms):
        mask = mask_of(c)
        columns = srcs[c].T
        sums = []
        for h in range(heads):
            logit = dsts[h] + columns[:, h : h + 1]
            up = logit > 0
            score = jnp.where(up, logit, 0.2 * logit)
            weight = jnp.where(mask, jnp.exp(score - peaks[h]), 0.0)
            sums.append(norms[h] + jnp.sum(weight, axis=0, keepdims=True))
            high, low = split(weight)
            w_hi[c, h] = high
            w_lo[c, h] = low
            w_slope[c, h] = jnp.where(up, weight, 0.2 * weight)
        return tuple(sums)

    zero_row = jnp.zeros((1, rows), f32)
    norms = lax.fori_loop(0, copies + 1, weight_step, (zero_row,) * heads)
    for turn in range(1, copies):
        feat_copy(mirror(turn)).wait_recv()
        far_copy(turn).start()
        near_copy(turn).start()
    feat_copy(2 * copies).wait_recv()
    for turn in range(1, copies):
        low_copy(turn).start()
    norms = lax.fori_loop(copies + 1, count, weight_step, norms)

    agg[...] = jnp.zeros(agg.shape, f32)

    def forward_step(c, carry):
        @pl.when(c == copies)
        def _():
            feat_copy(copies).wait_recv()

        @pl.when(jnp.logical_and(c > copies, c < 2 * copies))
        def _():
            near_copy(c - copies).wait_recv()

        @pl.when(c > 2 * copies)
        def _():
            far_copy(c - 2 * copies).wait_recv()
            low_copy(mirror(c - 2 * copies)).wait_recv()

        high, low = split(feats[c].T)
        both = jnp.concatenate([high, low], 1)
        for h in range(heads):
            part = pl.ds(h * head, head)
            w_h = w_hi[c, h]
            agg[part, :] += mm(both[h * head : (h + 1) * head], jnp.concatenate([w_h, w_h], 0)) + mm(
                high[h * head : (h + 1) * head], w_lo[c, h]
            )
        return carry

    lax.fori_loop(0, count, forward_step, 0)

    flat_source = jnp.sum(wide_source, axis=0, keepdims=True)
    left = lax.broadcasted_iota(jnp.int32, (rows, rows), 1) < head
    zero_half = jnp.zeros((head, rows), f32)
    zero_tile = jnp.zeros((rows, rows), f32)
    ones_tile = jnp.ones((rows, rows), f32)
    for p in range(pairs):
        scaled, outs = [], []
        for h in (2 * p, 2 * p + 1):
            inverse = 1.0 / norms[h]
            agg_t = agg[h * head : (h + 1) * head, :] * inverse
            raised = jnp.exp(jnp.minimum(agg_t, 0.0))
            outs.append(jnp.where(agg_t > 0, agg_t, raised - 1.0))
            g_t = cot_t[h * head : (h + 1) * head] * jnp.where(agg_t > 0, 1.0, raised)
            delta_s[h] = jnp.sum(g_t * agg_t, axis=0, keepdims=True) * inverse
            scaled.append(g_t * inverse)
        out_ref[:, p * 2 * head : (p + 1) * 2 * head] = jnp.concatenate(outs, 0).T
        g_pair = jnp.concatenate(scaled, 0).T
        block = jnp.concatenate(
            [
                jnp.concatenate([scaled[0], zero_half], 1),
                jnp.concatenate([zero_half, scaled[1]], 1),
            ],
            0,
        )
        high, low = split(block)
        probs_a[p] = jnp.concatenate([high, high], 0)
        probs_b[p] = low
        a_pair = jnp.broadcast_to(flat_source[:, p * 2 * head : (p + 1) * 2 * head], (rows, rows))
        mixed = jnp.concatenate(
            [
                jnp.concatenate([jnp.where(left, g_pair, 0.0), zero_tile], 1),
                jnp.concatenate(
                    [jnp.where(left, a_pair, 0.0), jnp.where(left, ones_tile, 0.0)], 1
                ),
                jnp.concatenate([jnp.where(left, 0.0, g_pair), zero_tile], 1),
                jnp.concatenate(
                    [jnp.where(left, 0.0, a_pair), jnp.where(left, 0.0, ones_tile)], 1
                ),
            ],
            0,
        )
        high, low = split(mixed)
        vals_hi[p] = high
        vals_lo[p] = low

    dst_sum[...] = jnp.zeros(dst_sum.shape, f32)
    src_att[...] = jnp.zeros(src_att.shape, f32)

    def backward_step(step, carry):
        c = lax.rem(step + 1, count)
        for p in range(pairs):
            tile = pl.ds(p * 2 * head, 2 * head)
            value = feats[c, :, tile]
            high, low = split(value)
            prob = mm(jnp.concatenate([high, low], 1), probs_a[p]) + mm(high, probs_b[p])
            highs, lows = [], []
            for side in range(2):
                h = 2 * p + side
                score = w_slope[c, h] * (prob[:, side * rows : (side + 1) * rows] - delta_s[h])
                dst_sum[h] += jnp.sum(score, axis=0, keepdims=True)
                s_hi, s_lo = split(score)
                highs += [w_hi[c, h], s_hi]
                lows += [w_lo[c, h], s_lo]
            left_hi = jnp.concatenate(highs, 1)
            left_lo = jnp.concatenate(lows, 1)
            both = mm(left_hi, vals_hi[p]) + mm(left_lo, vals_hi[p]) + mm(left_hi, vals_lo[p])
            sent[c, :, tile] = both[:, : 2 * head]
            src_att[p] += jnp.sum(both[:, 2 * head :] * value, axis=0, keepdims=True)

        @pl.when(c > 0)
        def _():
            grad_copy(c).start()

        return carry

    lax.fori_loop(0, count, backward_step, 0)

    dst_rows = jnp.concatenate([dst_sum[h] for h in range(heads)], 0)
    tgt_att = jnp.dot(dst_rows, feat_ref[...], precision=precise, preferred_element_type=f32)
    tgt_att = jnp.sum(jnp.where(on_head, tgt_att, 0.0), axis=0, keepdims=True)
    for p in range(pairs):
        red[blk, p : p + 1, :] = src_att[p]
        red[blk, pairs + p : pairs + p + 1, :] = tgt_att[:, p * 2 * head : (p + 1) * 2 * head]

    def red_copy(step, here):
        return pltpu.make_async_remote_copy(
            src_ref=red.at[here],
            dst_ref=red.at[here],
            send_sem=red_send.at[step],
            recv_sem=red_recv.at[here],
            device_id=(lax.rem(blk + step, cycle), cp),
            device_id_type=MESH,
        )

    def red_start(step, carry):
        red_copy(step, blk).start()
        return carry

    lax.fori_loop(1, cycle, red_start, 0)

    own_term = jnp.dot(dst_rows.T, wide_target, precision=precise, preferred_element_type=f32)
    grad_ref[...] = sent[0] + own_term

    def red_wait(step, carry):
        red_copy(step, lax.rem(blk + step, cycle)).wait_recv()
        return carry

    lax.fori_loop(1, cycle, red_wait, 0)
    total = red[0]
    for i in range(1, cycle):
        total = total + red[i]
    red2[cp] = total

    def red2_copy(turn, here):
        return pltpu.make_async_remote_copy(
            src_ref=red2.at[here],
            dst_ref=red2.at[here],
            send_sem=red2_send.at[turn],
            recv_sem=red2_recv.at[here],
            device_id=(blk, lax.rem(cp + turn, copies)),
            device_id_type=MESH,
        )

    for turn in range(1, copies):
        red2_copy(turn, cp).start()

    def grad_step(c, carry):
        grad_copy(mirror(c)).wait_recv()
        grad_ref[...] += got[c]
        return carry

    lax.fori_loop(1, count, grad_step, 0)

    for turn in range(1, copies):
        red2_copy(turn, lax.rem(cp + turn, copies)).wait_recv()
    total = red2[0]
    for i in range(1, copies):
        total = total + red2[i]
    for p in range(pairs):
        for side in range(2):
            h = 2 * p + side
            span = slice(side * head, (side + 1) * head)
            sgrad_ref[h : h + 1, :] = total[p : p + 1, span]
            tgrad_ref[h : h + 1, :] = total[pairs + p : pairs + p + 1, span]

    for c in range(1, count):
        src_copy(c).wait_send()
        grad_copy(c).wait_send()
    for c in direct:
        feat_copy(c).wait_send()
    for turn in range(1, copies):
        near_copy(turn).wait_send()
        far_copy(turn).wait_send()
        low_copy(turn).wait_send()

    def red_sent(step, carry):
        red_copy(step, blk).wait_send()
        return carry

    lax.fori_loop(1, cycle, red_sent, 0)
    for turn in range(1, copies):
        red2_copy(turn, cp).wait_send()


def settle(*refs):
    sems = refs[-1]
    count = len(refs) // 2
    moves = [
        pltpu.make_async_copy(refs[i], refs[count + i], sems.at[i]) for i in range(count)
    ]
    for move in moves:
        move.start()
    for move in moves:
        move.wait()


def per_device(
    features, attend_source, attend_target, key_blocks, live_slots, edge_bits, cotangent
):
    heads, head = attend_source.shape
    rows, width = features.shape
    copies = lax.axis_size("copy")
    cycle = lax.axis_size("blk")
    count = 3 * copies
    pairs = heads // 2
    slots, word_rows = edge_bits.shape[1:3]
    vmem = pl.BlockSpec(memory_space=pltpu.VMEM)
    hbm = pl.BlockSpec(memory_space=pltpu.HBM)
    anywhere = pl.BlockSpec(memory_space=pl.ANY)
    dma = pltpu.SemaphoreType.DMA
    shapes = (
        jax.ShapeDtypeStruct((rows, width), f32),
        jax.ShapeDtypeStruct((rows, width), f32),
        jax.ShapeDtypeStruct((heads, head), f32),
        jax.ShapeDtypeStruct((heads, head), f32),
    )
    found = pl.pallas_call(
        functools.partial(kernel, cycle, copies),
        out_shape=shapes,
        in_specs=[hbm] * 7,
        out_specs=(vmem,) * 4,
        scratch_shapes=[
            pltpu.VMEM((heads, head), f32),
            pltpu.VMEM((heads, head), f32),
            pltpu.VMEM((1, slots), jnp.int32),
            pltpu.VMEM((1, 1), jnp.int32),
            pltpu.VMEM((slots, word_rows, rows), jnp.int32),
            pltpu.VMEM((rows, width), f32),
            pltpu.VMEM((count, rows, width), f32),
            pltpu.VMEM((count, heads, rows), f32),
            pltpu.VMEM((count, word_rows, rows), jnp.int32),
            pltpu.VMEM((count, heads, rows, rows), bf16),
            pltpu.VMEM((count, heads, rows, rows), bf16),
            pltpu.VMEM((count, heads, rows, rows), f32),
            pltpu.VMEM((width, rows), f32),
            pltpu.VMEM((pairs, 2 * rows, 2 * rows), bf16),
            pltpu.VMEM((pairs, rows, 2 * rows), bf16),
            pltpu.VMEM((pairs, 4 * rows, 2 * rows), bf16),
            pltpu.VMEM((pairs, 4 * rows, 2 * rows), bf16),
            pltpu.VMEM((heads, 1, rows), f32),
            pltpu.VMEM((count, rows, width), f32),
            pltpu.VMEM((count, rows, width), f32),
            pltpu.VMEM((heads, 1, rows), f32),
            pltpu.VMEM((pairs, 1, 2 * head), f32),
            pltpu.VMEM((cycle, heads, 2 * head), f32),
            pltpu.VMEM((copies, heads, 2 * head), f32),
            dma((count,)),
            dma((count,)),
            dma((count,)),
            dma((count,)),
            dma((count,)),
            dma((count,)),
            dma((cycle,)),
            dma((cycle,)),
            dma((copies,)),
            dma((copies,)),
            dma((7,)),
            dma((copies,)),
            dma((copies,)),
            dma((copies,)),
            dma((copies,)),
        ],
        compiler_params=pltpu.CompilerParams(
            collective_id=0, has_side_effects=True, vmem_limit_bytes=63 * 1024 * 1024
        ),
    )(
        features,
        attend_source,
        attend_target,
        key_blocks,
        live_slots.reshape(1, 1),
        edge_bits.reshape(slots, word_rows, rows),
        cotangent,
    )
    return pl.pallas_call(
        settle,
        out_shape=shapes,
        in_specs=[vmem] * 4,
        out_specs=(anywhere,) * 4,
        scratch_shapes=[dma((4,))],
        compiler_params=pltpu.CompilerParams(vmem_limit_bytes=63 * 1024 * 1024),
    )(*found)


def solution(mesh):
    placed = (
        P(("blk", "copy"), None),
        P(),
        P(),
        P(("blk", "copy"), None),
        P(("blk", "copy")),
        P(("blk", "copy"), None, None, None),
        P(("blk", "copy"), None),
    )
    return jax.shard_map(
        per_device,
        mesh=mesh,
        in_specs=placed,
        out_specs=(P(("blk", "copy"), None), P(("blk", "copy"), None), P(), P()),
        check_vma=False,
    )
```

```python
import functools

import jax
import jax.numpy as jnp
from jax import lax
from jax.experimental import pallas as pl
from jax.experimental.pallas import tpu as pltpu
from jax.sharding import PartitionSpec as P

precise = lax.Precision.HIGHEST
MESH = pl.DeviceIdType.MESH
f32 = jnp.float32
bf16 = jnp.bfloat16


def split(value):
    high = value.astype(bf16)
    return high, (value - high.astype(f32)).astype(bf16)


def mm(left, right):
    return jnp.dot(left, right, preferred_element_type=f32)


def kernel(
    cycle,
    copies,
    feat_hbm,
    source_hbm,
    target_hbm,
    blocks_hbm,
    live_hbm,
    edges_hbm,
    cot_hbm,
    out_ref,
    grad_ref,
    sgrad_ref,
    tgrad_ref,
    source_ref,
    target_ref,
    blocks_ref,
    live_ref,
    edges_ref,
    cot_ref,
    feats,
    srcs,
    bits,
    w_hi,
    w_lo,
    w_slope,
    agg,
    probs_a,
    probs_b,
    vals_hi,
    vals_lo,
    delta_s,
    sent,
    got,
    dst_sum,
    src_att,
    red,
    red2,
    feat_send,
    feat_recv,
    src_send,
    src_recv,
    grad_send,
    grad_recv,
    red_send,
    red_recv,
    red2_send,
    red2_recv,
    local_sem,
    low_recv,
    near_send,
    far_send,
    low_send,
    glow_send,
    glow_recv,
):
    rows, width = feat_hbm.shape
    half = rows // 2
    feat_ref = feats.at[0]
    heads, head = source_ref.shape
    slots = edges_ref.shape[0]
    count = 3 * copies
    pairs = heads // 2
    blk = lax.axis_index("blk")
    cp = lax.axis_index("copy")

    def place(c):
        group, turn = c // copies, c % copies
        shift = ((group + 1) % 3 - 1) * (1 - 2 * lax.rem(blk, 2))
        return lax.rem(blk + shift + cycle, cycle), lax.rem(cp + turn, copies)

    def mirror(c):
        group, turn = c // copies, c % copies
        return group * copies + (copies - turn) % copies

    loads = [
        pltpu.make_async_copy(source, target, local_sem.at[i])
        for i, (source, target) in enumerate(
            (
                (feat_hbm, feat_ref),
                (source_hbm, source_ref),
                (target_hbm, target_ref),
                (blocks_hbm, blocks_ref),
                (live_hbm, live_ref),
                (edges_hbm, edges_ref),
                (cot_hbm, cot_ref),
            )
        )
    ]
    for load in loads:
        load.start()

    barrier = pltpu.get_barrier_semaphore()
    for c in range(1, count):
        pl.semaphore_signal(barrier, inc=1, device_id=place(c), device_id_type=MESH)

    def greet(step, carry):
        pl.semaphore_signal(
            barrier, inc=1, device_id=(lax.rem(blk + step, cycle), cp), device_id_type=MESH
        )
        return carry

    lax.fori_loop(2, cycle - 1, greet, 0)

    for load in loads[:3]:
        load.wait()
    lane = lax.broadcasted_iota(jnp.int32, (heads, width), 1)
    head_row = lax.broadcasted_iota(jnp.int32, (heads, width), 0)
    on_head = lane // head == head_row
    wide_source = jnp.where(on_head, jnp.concatenate([source_ref[...]] * heads, 1), 0.0)
    wide_target = jnp.where(on_head, jnp.concatenate([target_ref[...]] * heads, 1), 0.0)
    logits = lax.dot_general(
        jnp.concatenate([wide_source, wide_target], 0),
        feat_ref[...],
        (((1,), (1,)), ((), ())),
        precision=precise,
        preferred_element_type=f32,
    )
    srcs[0] = logits[:heads]
    dst = logits[heads:]

    pl.semaphore_wait(barrier, count - 1 + cycle - 3)

    def src_copy(c):
        return pltpu.make_async_remote_copy(
            src_ref=srcs.at[0],
            dst_ref=srcs.at[mirror(c)],
            send_sem=src_send.at[c],
            recv_sem=src_recv.at[mirror(c)],
            device_id=place(c),
            device_id_type=MESH,
        )

    def feat_copy(c):
        return pltpu.make_async_remote_copy(
            src_ref=feat_hbm,
            dst_ref=feats.at[mirror(c)],
            send_sem=feat_send.at[c],
            recv_sem=feat_recv.at[mirror(c)],
            device_id=place(c),
            device_id_type=MESH,
        )

    def near_copy(turn):
        return pltpu.make_async_remote_copy(
            src_ref=feats.at[turn],
            dst_ref=feats.at[copies + turn],
            send_sem=near_send.at[turn],
            recv_sem=feat_recv.at[copies + turn],
            device_id=place(copies),
            device_id_type=MESH,
        )

    def far_copy(turn):
        return pltpu.make_async_remote_copy(
            src_ref=feats.at[turn, pl.ds(0, half)],
            dst_ref=feats.at[2 * copies + turn, pl.ds(0, half)],
            send_sem=far_send.at[turn],
            recv_sem=feat_recv.at[2 * copies + turn],
            device_id=place(2 * copies),
            device_id_type=MESH,
        )

    def low_copy(turn):
        return pltpu.make_async_remote_copy(
            src_ref=feats.at[2 * copies, pl.ds(half, half)],
            dst_ref=feats.at[mirror(2 * copies + turn), pl.ds(half, half)],
            send_sem=low_send.at[turn],
            recv_sem=low_recv.at[mirror(turn)],
            device_id=place(turn),
            device_id_type=MESH,
        )

    def own_grad(turn):
        return pltpu.make_async_remote_copy(
            src_ref=sent.at[turn],
            dst_ref=got.at[mirror(turn)],
            send_sem=grad_send.at[turn],
            recv_sem=grad_recv.at[mirror(turn)],
            device_id=place(turn),
            device_id_type=MESH,
        )

    def near_grad(turn):
        return pltpu.make_async_remote_copy(
            src_ref=sent.at[copies + turn],
            dst_ref=got.at[copies + turn],
            send_sem=grad_send.at[copies + turn],
            recv_sem=grad_recv.at[copies + turn],
            device_id=place(copies),
            device_id_type=MESH,
        )

    def far_grad(turn):
        return pltpu.make_async_remote_copy(
            src_ref=sent.at[2 * copies + turn, pl.ds(0, half)],
            dst_ref=got.at[2 * copies + turn, pl.ds(0, half)],
            send_sem=grad_send.at[2 * copies + turn],
            recv_sem=grad_recv.at[2 * copies + turn],
            device_id=place(2 * copies),
            device_id_type=MESH,
        )

    def low_grad(turn):
        return pltpu.make_async_remote_copy(
            src_ref=sent.at[2 * copies + turn, pl.ds(half, half)],
            dst_ref=got.at[2 * copies + mirror(turn), pl.ds(half, half)],
            send_sem=glow_send.at[turn],
            recv_sem=glow_recv.at[mirror(turn)],
            device_id=place(turn),
            device_id_type=MESH,
        )

    def low_sum():
        return pltpu.make_async_remote_copy(
            src_ref=sent.at[2 * copies, pl.ds(half, half)],
            dst_ref=got.at[2 * copies, pl.ds(half, half)],
            send_sem=glow_send.at[0],
            recv_sem=glow_recv.at[0],
            device_id=place(2 * copies),
            device_id_type=MESH,
        )

    for c in range(1, count):
        src_copy(c).start()
    direct = list(range(1, copies)) + [2 * copies, copies]
    for c in direct:
        feat_copy(c).start()
    for load in loads[3:]:
        load.wait()

    live = live_ref[...]
    for c in range(count):
        there, turn = place(c)
        block = there * copies + turn
        words = jnp.zeros(bits.shape[1:], jnp.int32)
        for slot in range(slots):
            chosen = jnp.logical_and(blocks_ref[:, slot : slot + 1] == block, slot < live)
            words = words + edges_ref[slot] * jnp.where(chosen, 1, 0)
        bits[c] = words

    cot_t = cot_ref[...].T
    bit = lax.broadcasted_iota(jnp.int32, (rows // 8, 8, rows), 1)
    key_row = lax.broadcasted_iota(jnp.int32, (rows, rows), 0)
    query_lane = lax.broadcasted_iota(jnp.int32, (rows, rows), 1)

    def mask_of(c):
        words = jnp.broadcast_to(bits[c][:, None, :], (rows // 8, 8, rows))
        mask = jnp.bitwise_and(jnp.right_shift(words, bit), 1).reshape(rows, rows)
        self_edge = jnp.where(key_row == query_lane, jnp.where(c == 0, 1, 0), 0)
        return jnp.bitwise_or(mask, self_edge) > 0

    for c in range(1, count):
        src_copy(mirror(c)).wait_recv()

    def peak_step(c, peaks):
        mask = mask_of(c)
        columns = srcs[c].T
        found = []
        for h in range(heads):
            masked = jnp.where(mask, columns[:, h : h + 1], -jnp.inf)
            found.append(jnp.maximum(peaks[h], jnp.max(masked, axis=0, keepdims=True)))
        return tuple(found)

    start = tuple(jnp.full((1, rows), -jnp.inf, f32) for _ in range(heads))
    tops = lax.fori_loop(0, count, peak_step, start)
    dsts = [dst[h : h + 1] for h in range(heads)]
    peaks = []
    for h in range(heads):
        top = dsts[h] + tops[h]
        peaks.append(jnp.where(top > 0, top, 0.2 * top))

    def weight_step(c, norms):
        mask = mask_of(c)
        columns = srcs[c].T
        sums = []
        for h in range(heads):
            logit = dsts[h] + columns[:, h : h + 1]
            up = logit > 0
            score = jnp.where(up, logit, 0.2 * logit)
            weight = jnp.where(mask, jnp.exp(score - peaks[h]), 0.0)
            sums.append(norms[h] + jnp.sum(weight, axis=0, keepdims=True))
            high, low = split(weight)
            w_hi[c, h] = high
            w_lo[c, h] = low
            w_slope[c, h] = jnp.where(up, weight, 0.2 * weight)
        return tuple(sums)

    zero_row = jnp.zeros((1, rows), f32)
    norms = lax.fori_loop(0, copies + 1, weight_step, (zero_row,) * heads)
    for turn in range(1, copies):
        feat_copy(mirror(turn)).wait_recv()
        far_copy(turn).start()
        near_copy(turn).start()
    feat_copy(2 * copies).wait_recv()
    for turn in range(1, copies):
        low_copy(turn).start()
    norms = lax.fori_loop(copies + 1, count, weight_step, norms)

    agg[...] = jnp.zeros(agg.shape, f32)

    def forward_step(c, carry):
        @pl.when(c == copies)
        def _():
            feat_copy(copies).wait_recv()

        @pl.when(jnp.logical_and(c > copies, c < 2 * copies))
        def _():
            near_copy(c - copies).wait_recv()

        @pl.when(c > 2 * copies)
        def _():
            far_copy(c - 2 * copies).wait_recv()
            low_copy(mirror(c - 2 * copies)).wait_recv()

        high, low = split(feats[c].T)
        both = jnp.concatenate([high, low], 1)
        for h in range(heads):
            part = pl.ds(h * head, head)
            w_h = w_hi[c, h]
            agg[part, :] += mm(both[h * head : (h + 1) * head], jnp.concatenate([w_h, w_h], 0)) + mm(
                high[h * head : (h + 1) * head], w_lo[c, h]
            )
        return carry

    lax.fori_loop(0, count, forward_step, 0)

    flat_source = jnp.sum(wide_source, axis=0, keepdims=True)
    left = lax.broadcasted_iota(jnp.int32, (rows, rows), 1) < head
    zero_half = jnp.zeros((head, rows), f32)
    zero_tile = jnp.zeros((rows, rows), f32)
    ones_tile = jnp.ones((rows, rows), f32)
    for p in range(pairs):
        scaled, outs = [], []
        for h in (2 * p, 2 * p + 1):
            inverse = 1.0 / norms[h]
            agg_t = agg[h * head : (h + 1) * head, :] * inverse
            raised = jnp.exp(jnp.minimum(agg_t, 0.0))
            outs.append(jnp.where(agg_t > 0, agg_t, raised - 1.0))
            g_t = cot_t[h * head : (h + 1) * head] * jnp.where(agg_t > 0, 1.0, raised)
            delta_s[h] = jnp.sum(g_t * agg_t, axis=0, keepdims=True) * inverse
            scaled.append(g_t * inverse)
        out_ref[:, p * 2 * head : (p + 1) * 2 * head] = jnp.concatenate(outs, 0).T
        g_pair = jnp.concatenate(scaled, 0).T
        block = jnp.concatenate(
            [
                jnp.concatenate([scaled[0], zero_half], 1),
                jnp.concatenate([zero_half, scaled[1]], 1),
            ],
            0,
        )
        high, low = split(block)
        probs_a[p] = jnp.concatenate([high, high], 0)
        probs_b[p] = low
        a_pair = jnp.broadcast_to(flat_source[:, p * 2 * head : (p + 1) * 2 * head], (rows, rows))
        mixed = jnp.concatenate(
            [
                jnp.concatenate([jnp.where(left, g_pair, 0.0), zero_tile], 1),
                jnp.concatenate(
                    [jnp.where(left, a_pair, 0.0), jnp.where(left, ones_tile, 0.0)], 1
                ),
                jnp.concatenate([jnp.where(left, 0.0, g_pair), zero_tile], 1),
                jnp.concatenate(
                    [jnp.where(left, 0.0, a_pair), jnp.where(left, 0.0, ones_tile)], 1
                ),
            ],
            0,
        )
        high, low = split(mixed)
        vals_hi[p] = high
        vals_lo[p] = low

    dst_sum[...] = jnp.zeros(dst_sum.shape, f32)
    src_att[...] = jnp.zeros(src_att.shape, f32)

    def backward(c):
        for p in range(pairs):
            tile = pl.ds(p * 2 * head, 2 * head)
            value = feats[c, :, tile]
            high, low = split(value)
            prob = mm(jnp.concatenate([high, low], 1), probs_a[p]) + mm(high, probs_b[p])
            highs, lows = [], []
            for side in range(2):
                h = 2 * p + side
                score = w_slope[c, h] * (prob[:, side * rows : (side + 1) * rows] - delta_s[h])
                dst_sum[h] += jnp.sum(score, axis=0, keepdims=True)
                s_hi, s_lo = split(score)
                highs += [w_hi[c, h], s_hi]
                lows += [w_lo[c, h], s_lo]
            left_hi = jnp.concatenate(highs, 1)
            left_lo = jnp.concatenate(lows, 1)
            both = mm(left_hi, vals_hi[p]) + mm(left_lo, vals_hi[p]) + mm(left_hi, vals_lo[p])
            sent[c, :, tile] = both[:, : 2 * head]
            src_att[p] += jnp.sum(both[:, 2 * head :] * value, axis=0, keepdims=True)

    def far_step(turn, carry):
        backward(2 * copies + turn)
        low_grad(turn).start()
        far_grad(turn).start()
        return carry

    lax.fori_loop(1, copies, far_step, 0)

    def near_step(turn, carry):
        backward(copies + turn)
        near_grad(turn).start()
        return carry

    lax.fori_loop(1, copies, near_step, 0)
    backward(2 * copies)
    far_grad(0).start()

    def own_step(turn, carry):
        backward(turn)
        near_grad(turn).wait_recv()
        far_grad(turn).wait_recv()
        sent[turn] += got[copies + turn]
        sent[turn, :half] += got[2 * copies + turn, :half]
        own_grad(turn).start()
        return carry

    lax.fori_loop(1, copies, own_step, 0)
    for turn in range(1, copies):
        low_grad(mirror(turn)).wait_recv()
        sent[2 * copies, half:] += got[2 * copies + turn, half:]
    low_sum().start()
    backward(copies)
    near_grad(0).start()
    backward(0)

    dst_rows = jnp.concatenate([dst_sum[h] for h in range(heads)], 0)
    tgt_att = jnp.dot(dst_rows, feat_ref[...], precision=precise, preferred_element_type=f32)
    tgt_att = jnp.sum(jnp.where(on_head, tgt_att, 0.0), axis=0, keepdims=True)
    for p in range(pairs):
        red[blk, p : p + 1, :] = src_att[p]
        red[blk, pairs + p : pairs + p + 1, :] = tgt_att[:, p * 2 * head : (p + 1) * 2 * head]

    def red_copy(step, here):
        return pltpu.make_async_remote_copy(
            src_ref=red.at[here],
            dst_ref=red.at[here],
            send_sem=red_send.at[step],
            recv_sem=red_recv.at[here],
            device_id=(lax.rem(blk + step, cycle), cp),
            device_id_type=MESH,
        )

    def red_start(step, carry):
        red_copy(step, blk).start()
        return carry

    lax.fori_loop(1, cycle, red_start, 0)

    own_term = jnp.dot(dst_rows.T, wide_target, precision=precise, preferred_element_type=f32)
    grad_ref[...] = sent[0] + own_term

    def red_wait(step, carry):
        red_copy(step, lax.rem(blk + step, cycle)).wait_recv()
        return carry

    lax.fori_loop(1, cycle, red_wait, 0)
    total = red[0]
    for i in range(1, cycle):
        total = total + red[i]
    red2[cp] = total

    def red2_copy(turn, here):
        return pltpu.make_async_remote_copy(
            src_ref=red2.at[here],
            dst_ref=red2.at[here],
            send_sem=red2_send.at[turn],
            recv_sem=red2_recv.at[here],
            device_id=(blk, lax.rem(cp + turn, copies)),
            device_id_type=MESH,
        )

    for turn in range(1, copies):
        red2_copy(turn, cp).start()

    near_grad(0).wait_recv()
    far_grad(0).wait_recv()
    low_sum().wait_recv()
    grad_ref[...] += got[copies] + got[2 * copies]
    for turn in range(1, copies):
        own_grad(mirror(turn)).wait_recv()
        grad_ref[...] += got[turn]

    for turn in range(1, copies):
        red2_copy(turn, lax.rem(cp + turn, copies)).wait_recv()
    total = red2[0]
    for i in range(1, copies):
        total = total + red2[i]
    for p in range(pairs):
        for side in range(2):
            h = 2 * p + side
            span = slice(side * head, (side + 1) * head)
            sgrad_ref[h : h + 1, :] = total[p : p + 1, span]
            tgrad_ref[h : h + 1, :] = total[pairs + p : pairs + p + 1, span]

    for c in range(1, count):
        src_copy(c).wait_send()
    for c in direct:
        feat_copy(c).wait_send()
    for turn in range(1, copies):
        near_copy(turn).wait_send()
        far_copy(turn).wait_send()
        low_copy(turn).wait_send()
        own_grad(turn).wait_send()
        low_grad(turn).wait_send()
    for turn in range(copies):
        near_grad(turn).wait_send()
        far_grad(turn).wait_send()
    low_sum().wait_send()

    def red_sent(step, carry):
        red_copy(step, blk).wait_send()
        return carry

    lax.fori_loop(1, cycle, red_sent, 0)
    for turn in range(1, copies):
        red2_copy(turn, cp).wait_send()


def settle(*refs):
    sems = refs[-1]
    count = len(refs) // 2
    moves = [
        pltpu.make_async_copy(refs[i], refs[count + i], sems.at[i]) for i in range(count)
    ]
    for move in moves:
        move.start()
    for move in moves:
        move.wait()


def per_device(
    features, attend_source, attend_target, key_blocks, live_slots, edge_bits, cotangent
):
    heads, head = attend_source.shape
    rows, width = features.shape
    copies = lax.axis_size("copy")
    cycle = lax.axis_size("blk")
    count = 3 * copies
    pairs = heads // 2
    slots, word_rows = edge_bits.shape[1:3]
    vmem = pl.BlockSpec(memory_space=pltpu.VMEM)
    hbm = pl.BlockSpec(memory_space=pltpu.HBM)
    anywhere = pl.BlockSpec(memory_space=pl.ANY)
    dma = pltpu.SemaphoreType.DMA
    shapes = (
        jax.ShapeDtypeStruct((rows, width), f32),
        jax.ShapeDtypeStruct((rows, width), f32),
        jax.ShapeDtypeStruct((heads, head), f32),
        jax.ShapeDtypeStruct((heads, head), f32),
    )
    found = pl.pallas_call(
        functools.partial(kernel, cycle, copies),
        out_shape=shapes,
        in_specs=[hbm] * 7,
        out_specs=(vmem,) * 4,
        scratch_shapes=[
            pltpu.VMEM((heads, head), f32),
            pltpu.VMEM((heads, head), f32),
            pltpu.VMEM((1, slots), jnp.int32),
            pltpu.VMEM((1, 1), jnp.int32),
            pltpu.VMEM((slots, word_rows, rows), jnp.int32),
            pltpu.VMEM((rows, width), f32),
            pltpu.VMEM((count, rows, width), f32),
            pltpu.VMEM((count, heads, rows), f32),
            pltpu.VMEM((count, word_rows, rows), jnp.int32),
            pltpu.VMEM((count, heads, rows, rows), bf16),
            pltpu.VMEM((count, heads, rows, rows), bf16),
            pltpu.VMEM((count, heads, rows, rows), f32),
            pltpu.VMEM((width, rows), f32),
            pltpu.VMEM((pairs, 2 * rows, 2 * rows), bf16),
            pltpu.VMEM((pairs, rows, 2 * rows), bf16),
            pltpu.VMEM((pairs, 4 * rows, 2 * rows), bf16),
            pltpu.VMEM((pairs, 4 * rows, 2 * rows), bf16),
            pltpu.VMEM((heads, 1, rows), f32),
            pltpu.VMEM((count, rows, width), f32),
            pltpu.VMEM((count, rows, width), f32),
            pltpu.VMEM((heads, 1, rows), f32),
            pltpu.VMEM((pairs, 1, 2 * head), f32),
            pltpu.VMEM((cycle, heads, 2 * head), f32),
            pltpu.VMEM((copies, heads, 2 * head), f32),
            dma((count,)),
            dma((count,)),
            dma((count,)),
            dma((count,)),
            dma((count,)),
            dma((count,)),
            dma((cycle,)),
            dma((cycle,)),
            dma((copies,)),
            dma((copies,)),
            dma((7,)),
            dma((copies,)),
            dma((copies,)),
            dma((copies,)),
            dma((copies,)),
            dma((copies,)),
            dma((copies,)),
        ],
        compiler_params=pltpu.CompilerParams(
            collective_id=0, has_side_effects=True, vmem_limit_bytes=63 * 1024 * 1024
        ),
    )(
        features,
        attend_source,
        attend_target,
        key_blocks,
        live_slots.reshape(1, 1),
        edge_bits.reshape(slots, word_rows, rows),
        cotangent,
    )
    return pl.pallas_call(
        settle,
        out_shape=shapes,
        in_specs=[vmem] * 4,
        out_specs=(anywhere,) * 4,
        scratch_shapes=[dma((4,))],
        compiler_params=pltpu.CompilerParams(vmem_limit_bytes=63 * 1024 * 1024),
    )(*found)


def solution(mesh):
    placed = (
        P(("blk", "copy"), None),
        P(),
        P(),
        P(("blk", "copy"), None),
        P(("blk", "copy")),
        P(("blk", "copy"), None, None, None),
        P(("blk", "copy"), None),
    )
    return jax.shard_map(
        per_device,
        mesh=mesh,
        in_specs=placed,
        out_specs=(P(("blk", "copy"), None), P(("blk", "copy"), None), P(), P()),
        check_vma=False,
    )
```
